32 devices in a mesh: section: 4 (over y, x), tp: 8 (over z, core).
Axes of the slice: x: 2, y: 2, z: 4, core: 2. Of those that a mesh axis runs over, the one named last changes fastest.
Arguments:
- head_outputs: bfloat16 [4, 32, 8192], P('section', None, 'tp'), may hold values from -6 to 6
- residual: bfloat16 [4, 32, 8192], P('section', 'tp'), may hold values from -38 to 38
- out_weight: bfloat16 [8192, 8192], P('tp'), may hold values from -0.0625 to 0.0625
- norm_gain: bfloat16 [8192], replicated, may hold values from 0.099609375 to 1.8984375
- prior_peak: float32 [4], P('section'), may hold values from 6 to 48
- qkv_weight: bfloat16 [8192, 9216], P(None, 'tp'), may hold values from -0.0625 to 0.0625
Outputs:
- stream: bfloat16 [4, 32, 8192], P('section', 'tp')
- projected: bfloat16 [4, 32, 9216], P('section', None, 'tp')
- group_peak: float32 [4], P('section')
The draws below stay inside these ranges and needn't reach their ends.
All inputs are finite; a program needn't handle non-finite values.
Results may differ from the reference program's by a relative error of at most 0.02.
Values may be sent and summed in bfloat16 or wider, within the bound.
A program may use at most 64 MiB of HBM per device.

```python
import math
import jax
import jax.numpy as jnp
from jax import lax

D = 8192
HQ = 64
HD = 128
TOK = 32
SECTIONS = 4
QKV = 9216
N_TP = 8


def draw_residual(key, part):
    first_key, second_key = jax.random.split(jax.random.fold_in(key, 11))
    bulk = jax.random.truncated_normal(first_key, -6.0, 6.0, (SECTIONS, TOK, D), jnp.float32)
    channel = jax.random.randint(second_key, (SECTIONS, TOK, 1), 0, D)
    position = jnp.arange(TOK).astype(jnp.float32) / max(TOK - 1, 1)
    amplitude = 8.0 * jnp.power(4.0, position)
    onehot = (jnp.arange(D)[None, None, :] == channel).astype(jnp.float32)
    return (bulk + onehot * amplitude[None, :, None]).astype(jnp.bfloat16)


def raised(array, rng, source, target, parts, factor):
    owner, partner = [(jnp.arange(array.shape[dim]) // (array.shape[dim] // parts)).reshape([-1 if axis == dim else 1 for axis in range(array.ndim)]) for dim in (source, target)]
    chosen = jax.random.permutation(rng, parts)[partner]
    strong = (owner == chosen) | (owner == (partner + parts // 2) % parts)
    return jnp.where(strong, factor * array, array)


def levels(own_key, dims, cuts, least, high):
    level, own = 1.0, jax.random.fold_in(own_key, 6)
    for axis_at, parts in cuts:
        steps = jnp.exp(jax.random.uniform(jax.random.fold_in(own, axis_at), (parts,), jnp.float32, least / len(cuts), high / len(cuts)))
        level = level * jnp.repeat(steps, dims[axis_at] // parts).reshape([-1 if axis == axis_at else 1 for axis in range(len(dims))])
    return level


def noise(rng, shape, width, limit, pieces=(), kind=jnp.bfloat16):
    entries = jax.random.normal(rng, shape, jnp.float32) * width
    if len(pieces) > 0:
        entries = levels(rng, shape, pieces, -0.22, 0.18) * entries
    return jnp.clip(entries, min=-limit, max=limit).astype(kind)


def noise_with(rng, extent, deviation, limit, cuts, heavy, held_as=jnp.bfloat16):
    array = deviation * jax.random.normal(rng, extent, jnp.float32)
    if cuts:
        array = array * levels(rng, extent, cuts, -0.22, 0.18)
    return jnp.clip(raised(array, jax.random.fold_in(rng, 3), *heavy), -limit, limit).astype(held_as)


def setup_inputs(seed: int = 0) -> dict:
    key_list = jax.random.split(jax.random.key(seed), 7)
    return {
        "head_outputs": noise_with(key_list[0], (SECTIONS, TOK, HQ * HD), 1.0, 6.0, ((0, 4), (2, 8)), (2, 1, 8, 2.0)),
        "residual": draw_residual(jax.random.fold_in(key_list[6], 71), 0),
        "out_weight": noise(key_list[2], (HQ * HD, D), (HQ * HD) ** -0.5, 0.0625, ((0, 8),)),
        "norm_gain": jnp.clip(1.0 + 0.18 * jax.random.normal(key_list[3], (D,), jnp.float32), 0.099609375, 1.8984375).astype(jnp.bfloat16),
        "prior_peak": jnp.clip(jnp.exp(math.log(48.0) - 2.0794415 * jax.random.uniform(key_list[4], (SECTIONS,), jnp.float32) ** levels(key_list[4], (SECTIONS,), ((0, 4),), -0.2, 0.2)), 6.0, 48.0),
        "qkv_weight": noise(key_list[5], (D, QKV), D ** -0.5, 0.0625, ((1, 8),)),
    }


epsilon = 1e-05
ceiling = 448.0

def normalize(stream_rows, norm_gain):
    widened = stream_rows.astype(jnp.float32)
    mean_square = lax.optimization_barrier(jnp.mean(widened * widened, axis=-1, keepdims=True))
    return widened * lax.rsqrt(mean_square + epsilon) * norm_gain.astype(jnp.float32)

def reference(head_outputs, residual, out_weight, norm_gain, prior_peak, qkv_weight):
    head_width = HQ * HD // N_TP
    blocks = out_weight.reshape(N_TP, head_width, D)

    def section_forward(inputs):
        heads_section, resid_section, peak_section = inputs
        split_heads = heads_section.reshape(TOK, N_TP, head_width).transpose(1, 0, 2)

        def accumulate(running, paired):
            portion, weight_block = paired
            partial_value = jnp.dot(portion, weight_block, preferred_element_type=jnp.float32)
            rounded = lax.optimization_barrier(partial_value.astype(jnp.bfloat16))
            return (running + rounded.astype(jnp.float32), None)
        summed, unused = lax.scan(accumulate, jnp.zeros((TOK, D), jnp.float32), (split_heads, blocks))
        stream = (resid_section.astype(jnp.float32) + summed).astype(jnp.bfloat16)
        normed = normalize(stream, norm_gain)
        scale_unit = (peak_section / ceiling).astype(jnp.bfloat16)
        quantized = jnp.clip(normed / scale_unit.astype(jnp.float32), -ceiling, ceiling).astype(jnp.bfloat16)
        peak_value = jnp.max(jnp.abs(normed))
        return (stream, quantized, scale_unit, peak_value)
    stream, quantized, scale_unit, peak_value = lax.map(section_forward, (head_outputs, residual, prior_peak))
    arrived = jnp.roll(quantized, 1, axis=0)
    arrived_unit = jnp.roll(scale_unit, 1, axis=0)

    def project(inputs):
        arrived_rows, unit_in = inputs
        product = jnp.dot(arrived_rows, qkv_weight, preferred_element_type=jnp.float32)
        return (product * unit_in.astype(jnp.float32)).astype(jnp.bfloat16)
    projected = lax.map(project, (arrived, arrived_unit))
    return (stream, projected, peak_value)
```

```python
import functools

import jax
import jax.numpy as jnp
from jax import lax
from jax.experimental import pallas as pl
from jax.experimental.pallas import tpu as pltpu
from jax.sharding import PartitionSpec as P

EPSILON = 1e-05
CEILING = 448.0
CORES = 2
TILE = 16
CHUNKS = 4
MESH = pl.DeviceIdType.MESH


def one_hot(shape, column_of_row):
    rows = lax.broadcasted_iota(jnp.int32, shape, 0)
    columns = lax.broadcasted_iota(jnp.int32, shape, 1)
    return jnp.where(columns == column_of_row(rows), 1.0, 0.0).astype(jnp.bfloat16)


def permuted(matrix, x):
    return jnp.dot(matrix, x, preferred_element_type=jnp.float32).astype(jnp.bfloat16)


def kernel(
    sections, tp,
    heads_hbm, resid_ref, w1_hbm, gain_ref, prior_ref, w2_hbm,
    stream_ref, proj_ref, peak_ref,
    heads, w1, w2, own, pair_send, pair_recv, rs_send, rs_recv, slab, gains,
    ag_send, ag_recv, peaks,
    heads_sem, w1_sem, w2_sem, pair_ssem, pair_rsem, rs_ssem, rs_rsem,
    ag_ssem, ag_rsem, fw_ssem, fw_rsem, peak_ssem, peak_rsem,
):
    s = lax.axis_index("section")
    t = lax.axis_index("tp")
    zs = tp // CORES
    z = t // CORES
    c = t % CORES
    other = 1 - c
    partner = (s, z * CORES + other)
    after = lax.rem(s + 1, sections)
    before = lax.rem(s + sections - 1, sections)
    tokens = heads.shape[0]
    r = tokens // tp
    parts = TILE // r
    width = w1.shape[1]
    q = width // parts
    w = q // CHUNKS
    half = zs * r

    def at(zz, cc):
        return zz * CORES + cc

    heads_copy = pltpu.make_async_copy(heads_hbm, heads, heads_sem)
    heads_copy.start()
    w1_copies = []
    for k in range(CHUNKS):
        for j in range(parts):
            cols = pl.ds(j * q + k * w, w)
            cp = pltpu.make_async_copy(w1_hbm.at[:, cols], w1.at[:, cols], w1_sem.at[k, j])
            cp.start()
            w1_copies.append(cp)

    barrier = pltpu.get_barrier_semaphore()
    for d in range(1, tp):
        pl.semaphore_signal(barrier, inc=1, device_id=(s, lax.rem(t + d, tp)), device_id_type=MESH)
    for zz in range(zs):
        pl.semaphore_signal(barrier, inc=1, device_id=(before, at(zz, c)), device_id_type=MESH)

    for j in range(parts):
        cols = slice(j * q, (j + 1) * q)
        rows = slice(j * r, (j + 1) * r)
        slab[rows, :] = resid_ref[:, cols].astype(jnp.float32)
        gains[rows, :] = jnp.broadcast_to(gain_ref[:, cols].astype(jnp.float32), (r, q))

    to_halves = one_hot(
        (tokens, tokens),
        lambda p: (((p % half) // r) * CORES + (c + p // half) % CORES) * r + p % r,
    )
    to_slabs = one_hot(
        (parts * half, parts * half),
        lambda p: ((p % TILE) // r) * half + (p // TILE) * r + p % r,
    )

    heads_copy.wait()
    heads[...] = permuted(to_halves, heads[...])

    pair_copies, rs_copies = [], []

    def reduce_chunk(k):
        cols = slice(k * w, (k + 1) * w)
        pair_copies[k].wait_recv()
        total = (own[:, cols] + pair_recv[k].astype(jnp.float32)).astype(jnp.bfloat16)
        turned = permuted(to_slabs, total)
        for zz in range(zs):
            rs_send[k, zz] = turned[zz * TILE:(zz + 1) * TILE]
        for d in range(1, zs):
            zz = lax.rem(z + d, zs)
            cp = pltpu.make_async_remote_copy(
                src_ref=rs_send.at[k, zz], dst_ref=rs_recv.at[k, z],
                send_sem=rs_ssem.at[k, zz], recv_sem=rs_rsem.at[k, z],
                device_id=(s, at(zz, c)), device_id_type=MESH)
            cp.start()
            rs_copies.append(cp)

    w2_copies = []
    for k in range(CHUNKS):
        for j in range(parts):
            w1_copies[k * parts + j].wait()
        for j in range(parts):
            rows = pl.ds(j * q + k * w, w)
            cp = pltpu.make_async_copy(w2_hbm.at[rows], w2.at[rows], w2_sem.at[k, j])
            cp.start()
            w2_copies.append(cp)
        for j in range(parts):
            product = jnp.dot(heads[...], w1[:, j * q + k * w:j * q + (k + 1) * w],
                              preferred_element_type=jnp.float32)
            rows = slice(j * half, (j + 1) * half)
            own[rows, k * w:(k + 1) * w] = product[:half]
            pair_send[k, rows, :] = product[half:].astype(jnp.bfloat16)
        if k == 0:
            pl.semaphore_wait(barrier, tp - 1 + zs)
        cp = pltpu.make_async_remote_copy(
            src_ref=pair_send.at[k], dst_ref=pair_recv.at[k],
            send_sem=pair_ssem.at[k], recv_sem=pair_rsem.at[k],
            device_id=partner, device_id_type=MESH)
        cp.start()
        pair_copies.append(cp)
        if k >= 1:
            reduce_chunk(k - 1)
    reduce_chunk(CHUNKS - 1)

    squares = jnp.zeros((TILE, 1), jnp.float32)
    for k in range(CHUNKS):
        cols = slice(k * w, (k + 1) * w)
        total = rs_send[k, z].astype(jnp.float32)
        for d in range(1, zs):
            zz = lax.rem(z + d, zs)
            pltpu.make_async_remote_copy(
                src_ref=rs_send.at[k, zz], dst_ref=rs_recv.at[k, zz],
                send_sem=rs_ssem.at[k, zz], recv_sem=rs_rsem.at[k, zz],
                device_id=(s, at(zz, c)), device_id_type=MESH).wait_recv()
            total = total + rs_recv[k, zz].astype(jnp.float32)
        rounded = (slab[:, cols] + total).astype(jnp.bfloat16).astype(jnp.float32)
        slab[:, cols] = rounded
        squares = squares + jnp.sum(rounded * rounded, axis=1, keepdims=True)

    row_sum = squares[0:r]
    for j in range(1, parts):
        row_sum = row_sum + squares[j * r:(j + 1) * r]
    inverse = lax.rsqrt(row_sum / width + EPSILON)
    inverse = jnp.concatenate([inverse] * parts, axis=0)
    unit = (jnp.full((1, 1), prior_ref[0]) / CEILING).astype(jnp.bfloat16).astype(jnp.float32)
    limit = unit * CEILING

    ag_copies = []
    highest = jnp.zeros((TILE, w), jnp.float32)
    for k in range(CHUNKS):
        cols = slice(k * w, (k + 1) * w)
        normed = slab[:, cols] * inverse * gains[:, cols]
        highest = jnp.maximum(highest, jnp.abs(normed))
        ag_send[k] = jnp.clip(normed, -limit, limit).astype(jnp.bfloat16)
        for d in range(zs):
            zz = lax.rem(z + d + 1, zs)
            cp = pltpu.make_async_remote_copy(
                src_ref=ag_send.at[k], dst_ref=ag_recv.at[k, t],
                send_sem=ag_ssem.at[k, zz], recv_sem=ag_rsem.at[k, z],
                device_id=(after, at(zz, c)), device_id_type=MESH)
            cp.start()
            ag_copies.append(cp)

    peaks[t] = jnp.full(peaks.shape[1:], jnp.max(highest), jnp.float32)
    peak_copies = []
    for d in range(1, tp):
        tt = lax.rem(t + d, tp)
        cp = pltpu.make_async_remote_copy(
            src_ref=peaks.at[t], dst_ref=peaks.at[t],
            send_sem=peak_ssem.at[tt], recv_sem=peak_rsem.at[t],
            device_id=(s, tt), device_id_type=MESH)
        cp.start()
        peak_copies.append(cp)

    for j in range(parts):
        stream_ref[:, j * q:(j + 1) * q] = slab[j * r:(j + 1) * r, :].astype(jnp.bfloat16)

    to_tokens = [
        one_hot((tokens, tp * TILE), lambda p, j=j: (p // r) * TILE + j * r + p % r)
        for j in range(parts)
    ]

    fw_copies = []
    acc = jnp.zeros(proj_ref.shape, jnp.float32)

    def project_chunk(k, acc):
        for d in range(zs):
            zz = lax.rem(z + d, zs)
            pltpu.make_async_remote_copy(
                src_ref=ag_recv.at[k, at(zz, other)], dst_ref=ag_recv.at[k, at(zz, other)],
                send_sem=fw_ssem.at[k, zz], recv_sem=fw_rsem.at[k, zz],
                device_id=partner, device_id_type=MESH).wait_recv()
        rows = ag_recv[k].reshape(tp * TILE, w)
        for j in range(parts):
            w2_copies[k * parts + j].wait()
            acc = acc + jnp.dot(permuted(to_tokens[j], rows),
                                w2[j * q + k * w:j * q + (k + 1) * w, :],
                                preferred_element_type=jnp.float32)
        return acc

    for k in range(CHUNKS):
        for d in range(zs):
            zz = lax.rem(z + zs - d, zs)
            pltpu.make_async_remote_copy(
                src_ref=ag_send.at[k], dst_ref=ag_recv.at[k, at(zz, c)],
                send_sem=ag_ssem.at[k, zz], recv_sem=ag_rsem.at[k, zz],
                device_id=(after, at(zz, c)), device_id_type=MESH).wait_recv()
            cp = pltpu.make_async_remote_copy(
                src_ref=ag_recv.at[k, at(zz, c)], dst_ref=ag_recv.at[k, at(zz, c)],
                send_sem=fw_ssem.at[k, zz], recv_sem=fw_rsem.at[k, zz],
                device_id=partner, device_id_type=MESH)
            cp.start()
            fw_copies.append(cp)
        if k >= 1:
            acc = project_chunk(k - 1, acc)
    acc = project_chunk(CHUNKS - 1, acc)
    proj_ref[...] = acc.astype(jnp.bfloat16)

    for d in range(1, tp):
        tt = lax.rem(t + d, tp)
        pltpu.make_async_remote_copy(
            src_ref=peaks.at[tt], dst_ref=peaks.at[tt],
            send_sem=peak_ssem.at[tt], recv_sem=peak_rsem.at[tt],
            device_id=(s, tt), device_id_type=MESH).wait_recv()
    peak_ref[0] = jnp.max(peaks[...])

    for cp in pair_copies + rs_copies + ag_copies + fw_copies + peak_copies:
        cp.wait_send()


def shards(sections, tp, head_outputs, residual, out_weight, norm_gain, prior_peak, qkv_weight):
    heads, resid = head_outputs[0], residual[0]
    tokens, depth = heads.shape
    width = out_weight.shape[1]
    columns = qkv_weight.shape[1]
    r = resid.shape[0]
    zs = tp // CORES
    parts = TILE // r
    q = width // parts
    w = q // CHUNKS
    bf16, f32 = jnp.bfloat16, jnp.float32
    vmem, hbm, smem = (pl.BlockSpec(memory_space=m) for m in (pltpu.VMEM, pltpu.HBM, pltpu.SMEM))
    dma = pltpu.SemaphoreType.DMA
    flops = 2 * tokens * width * (depth + columns)
    stream, projected, peak = pl.pallas_call(
        functools.partial(kernel, sections, tp),
        out_shape=(
            jax.ShapeDtypeStruct((r, width), bf16),
            jax.ShapeDtypeStruct((tokens, columns), bf16),
            jax.ShapeDtypeStruct((1,), f32),
        ),
        in_specs=[hbm, vmem, hbm, vmem, smem, hbm],
        out_specs=(vmem, vmem, smem),
        scratch_shapes=[
            pltpu.VMEM((tokens, depth), bf16),
            pltpu.VMEM((depth, width), bf16),
            pltpu.VMEM((width, columns), bf16),
            pltpu.VMEM((parts * zs * r, q), f32),
            pltpu.VMEM((CHUNKS, parts * zs * r, w), bf16),
            pltpu.VMEM((CHUNKS, parts * zs * r, w), bf16),
            pltpu.VMEM((CHUNKS, zs, TILE, w), bf16),
            pltpu.VMEM((CHUNKS, zs, TILE, w), bf16),
            pltpu.VMEM((TILE, q), f32),
            pltpu.VMEM((TILE, q), f32),
            pltpu.VMEM((CHUNKS, TILE, w), bf16),
            pltpu.VMEM((CHUNKS, tp, TILE, w), bf16),
            pltpu.VMEM((tp, 8, 128), f32),
            dma, dma((CHUNKS, parts)), dma((CHUNKS, parts)),
            dma((CHUNKS,)), dma((CHUNKS,)),
            dma((CHUNKS, zs)), dma((CHUNKS, zs)),
            dma((CHUNKS, zs)), dma((CHUNKS, zs)),
            dma((CHUNKS, zs)), dma((CHUNKS, zs)),
            dma((tp,)), dma((tp,)),
        ],
        compiler_params=pltpu.CompilerParams(
            collective_id=0, has_side_effects=True, vmem_limit_bytes=48 * 1024 * 1024),
        cost_estimate=pl.CostEstimate(
            flops=flops, bytes_accessed=2 * width * (depth + columns), transcendentals=0),
    )(heads, resid, out_weight, norm_gain.reshape(1, width), prior_peak, qkv_weight)
    return stream[None], projected[None], peak


def solution(mesh):
    sections, tp = mesh.shape["section"], mesh.shape["tp"]
    return jax.shard_map(
        functools.partial(shards, sections, tp),
        mesh=mesh,
        in_specs=(
            P("section", None, "tp"),
            P("section", "tp", None),
            P("tp", None),
            P(),
            P("section"),
            P(None, "tp"),
        ),
        out_specs=(P("section", "tp", None), P("section", None, "tp"), P("section")),
        check_vma=False,
    )
```

```python
import functools

import jax
import jax.numpy as jnp
from jax import lax
from jax.experimental import pallas as pl
from jax.experimental.pallas import tpu as pltpu
from jax.sharding import PartitionSpec as P

EPSILON = 1e-05
CEILING = 448.0
CORES = 2
TILE = 16
CHUNKS = 4
LATE = 1
W2_AFTER = 2
VMEM_BYTES = 52 * 1024 * 1024
MESH = pl.DeviceIdType.MESH


def one_hot(shape, column_of_row):
    rows = lax.broadcasted_iota(jnp.int32, shape, 0)
    columns = lax.broadcasted_iota(jnp.int32, shape, 1)
    return jnp.where(columns == column_of_row(rows), 1.0, 0.0).astype(jnp.bfloat16)


def permuted(matrix, x):
    return jnp.dot(matrix, x, preferred_element_type=jnp.float32).astype(jnp.bfloat16)


def local(kind, source, target, semaphore):
    return pltpu.make_async_copy(source, target, semaphore)


def remote(kind, source, target, sent, received, device):
    return pltpu.make_async_remote_copy(
        src_ref=source, dst_ref=target, send_sem=sent, recv_sem=received,
        device_id=device, device_id_type=MESH)


def kernel(
    sections, tp,
    heads_ref, resid_hbm, w1_hbm, gain_hbm, prior_ref, w2_hbm,
    stream_ref, proj_ref, peak_ref,
    heads, resid, gain, w1, w2, own, pair_send, pair_recv, rs_send, rs_recv, slab, gains,
    ag_send, ag_recv, peaks,
    resid_sem, gain_sem, w1_sem, w2_sem, pair_ssem, pair_rsem, rs_ssem, rs_rsem,
    ag_ssem, ag_rsem, fw_ssem, fw_rsem, peak_ssem, peak_rsem,
):
    s = lax.axis_index("section")
    t = lax.axis_index("tp")
    zs = tp // CORES
    z = t // CORES
    c = t % CORES
    other = 1 - c
    partner = (s, z * CORES + other)
    after = lax.rem(s + 1, sections)
    before = lax.rem(s + sections - 1, sections)
    tokens = heads.shape[0]
    r = tokens // tp
    parts = TILE // r
    width = w1.shape[1]
    q = width // parts
    w, v = q // CHUNKS, q // LATE
    half = zs * r

    def at(zz, cc):
        return zz * CORES + cc

    w1_copies = []
    for k in range(CHUNKS):
        for j in range(parts):
            cols = pl.ds(j * q + k * w, w)
            cp = local("w1", w1_hbm.at[:, cols], w1.at[:, cols], w1_sem.at[k, j])
            cp.start()
            w1_copies.append(cp)
        if k == 0:
            resid_copy = local("in", resid_hbm, resid, resid_sem)
            gain_copy = local("in", gain_hbm, gain, gain_sem)
            resid_copy.start()
            gain_copy.start()

    barrier = pltpu.get_barrier_semaphore()
    for d in range(1, tp):
        pl.semaphore_signal(barrier, inc=1, device_id=(s, lax.rem(t + d, tp)), device_id_type=MESH)
    for zz in range(zs):
        pl.semaphore_signal(barrier, inc=1, device_id=(before, at(zz, c)), device_id_type=MESH)

    to_halves = one_hot(
        (tokens, tokens),
        lambda p: (((p % half) // r) * CORES + (c + p // half) % CORES) * r + p % r,
    )
    to_slabs = one_hot(
        (parts * half, parts * half),
        lambda p: ((p % TILE) // r) * half + (p // TILE) * r + p % r,
    )

    heads[...] = permuted(to_halves, heads_ref[...])

    pair_copies, rs_copies = [], []

    def reduce_chunk(k):
        cols = slice(k * w, (k + 1) * w)
        pair_copies[k].wait_recv()
        total = (own[:, cols] + pair_recv[k].astype(jnp.float32)).astype(jnp.bfloat16)
        turned = permuted(to_slabs, total)
        for zz in range(zs):
            rs_send[k, zz] = turned[zz * TILE:(zz + 1) * TILE]
        for d in range(1, zs):
            zz = lax.rem(z + d, zs)
            cp = remote("rs", rs_send.at[k, zz], rs_recv.at[k, z], rs_ssem.at[k, zz], rs_rsem.at[k, z], (s, at(zz, c)))
            cp.start()
            rs_copies.append(cp)

    w2_copies = []
    for k in range(CHUNKS):
        for j in range(parts):
            w1_copies[k * parts + j].wait()
        if k == W2_AFTER:
            for n in range(LATE):
                for j in range(parts):
                    rows = pl.ds(j * q + n * v, v)
                    cp = local("w2", w2_hbm.at[rows], w2.at[rows], w2_sem.at[n, j])
                    cp.start()
                    w2_copies.append(cp)
        for j in range(parts):
            product = jnp.dot(heads[...], w1[:, j * q + k * w:j * q + (k + 1) * w],
                              preferred_element_type=jnp.float32)
            rows = slice(j * half, (j + 1) * half)
            own[rows, k * w:(k + 1) * w] = product[:half]
            pair_send[k, rows, :] = product[half:].astype(jnp.bfloat16)
        if k == 0:
            pl.semaphore_wait(barrier, tp - 1 + zs)
        cp = remote("pair", pair_send.at[k], pair_recv.at[k], pair_ssem.at[k], pair_rsem.at[k], partner)
        cp.start()
        pair_copies.append(cp)
        if k >= 1:
            reduce_chunk(k - 1)
    reduce_chunk(CHUNKS - 1)

    resid_copy.wait()
    gain_copy.wait()
    gain_row = gain[...].astype(jnp.float32).reshape(1, width)
    for j in range(parts):
        cols = slice(j * q, (j + 1) * q)
        rows = slice(j * r, (j + 1) * r)
        slab[rows, :] = resid[:, cols].astype(jnp.float32)
        gains[rows, :] = jnp.broadcast_to(gain_row[:, cols], (r, q))

    squares = jnp.zeros((TILE, 1), jnp.float32)
    for k in range(CHUNKS):
        cols = slice(k * w, (k + 1) * w)
        total = rs_send[k, z].astype(jnp.float32)
        for d in range(1, zs):
            zz = lax.rem(z + d, zs)
            remote("rs", rs_send.at[k, zz], rs_recv.at[k, zz], rs_ssem.at[k, zz], rs_rsem.at[k, zz], (s, at(zz, c))).wait_recv()
            total = total + rs_recv[k, zz].astype(jnp.float32)
        rounded = (slab[:, cols] + total).astype(jnp.bfloat16).astype(jnp.float32)
        slab[:, cols] = rounded
        squares = squares + jnp.sum(rounded * rounded, axis=1, keepdims=True)

    row_sum = squares[0:r]
    for j in range(1, parts):
        row_sum = row_sum + squares[j * r:(j + 1) * r]
    inverse = lax.rsqrt(row_sum / width + EPSILON)
    inverse = jnp.concatenate([inverse] * parts, axis=0)
    unit = (jnp.full((1, 1), prior_ref[0]) / CEILING).astype(jnp.bfloat16).astype(jnp.float32)
    limit = unit * CEILING

    ag_copies = []
    highest = jnp.zeros((TILE, v), jnp.float32)
    for k in range(LATE):
        cols = slice(k * v, (k + 1) * v)
        normed = slab[:, cols] * inverse * gains[:, cols]
        highest = jnp.maximum(highest, jnp.abs(normed))
        ag_send[k] = jnp.clip(normed, -limit, limit).astype(jnp.bfloat16)
        for d in range(zs):
            zz = lax.rem(z + d + 1, zs)
            cp = remote("ag", ag_send.at[k], ag_recv.at[k, t], ag_ssem.at[k, zz], ag_rsem.at[k, z], (after, at(zz, c)))
            cp.start()
            ag_copies.append(cp)

    peaks[t] = jnp.full(peaks.shape[1:], jnp.max(highest), jnp.float32)
    peak_copies = []
    for d in range(1, tp):
        tt = lax.rem(t + d, tp)
        cp = remote("peak", peaks.at[t], peaks.at[t], peak_ssem.at[tt], peak_rsem.at[t], (s, tt))
        cp.start()
        peak_copies.append(cp)

    for j in range(parts):
        stream_ref[:, j * q:(j + 1) * q] = slab[j * r:(j + 1) * r, :].astype(jnp.bfloat16)

    to_tokens = [
        one_hot((tokens, tp * TILE), lambda p, j=j: (p // r) * TILE + j * r + p % r)
        for j in range(parts)
    ]

    fw_copies = []
    acc = jnp.zeros(proj_ref.shape, jnp.float32)

    def project_chunk(k, acc):
        for d in range(zs):
            zz = lax.rem(z + d, zs)
            remote("fw", ag_recv.at[k, at(zz, other)], ag_recv.at[k, at(zz, other)], fw_ssem.at[k, zz], fw_rsem.at[k, zz], partner).wait_recv()
        rows = ag_recv[k].reshape(tp * TILE, v)
        for j in range(parts):
            w2_copies[k * parts + j].wait()
            acc = acc + jnp.dot(permuted(to_tokens[j], rows),
                                w2[j * q + k * v:j * q + (k + 1) * v, :],
                                preferred_element_type=jnp.float32)
        return acc

    for k in range(LATE):
        for d in range(zs):
            zz = lax.rem(z + zs - d, zs)
            remote("ag", ag_send.at[k], ag_recv.at[k, at(zz, c)], ag_ssem.at[k, zz], ag_rsem.at[k, zz], (after, at(zz, c))).wait_recv()
            cp = remote("fw", ag_recv.at[k, at(zz, c)], ag_recv.at[k, at(zz, c)], fw_ssem.at[k, zz], fw_rsem.at[k, zz], partner)
            cp.start()
            fw_copies.append(cp)
        if k >= 1:
            acc = project_chunk(k - 1, acc)
    acc = project_chunk(LATE - 1, acc)
    proj_ref[...] = acc.astype(jnp.bfloat16)

    for d in range(1, tp):
        tt = lax.rem(t + d, tp)
        remote("peak", peaks.at[tt], peaks.at[tt], peak_ssem.at[tt], peak_rsem.at[tt], (s, tt)).wait_recv()
    peak_ref[0] = jnp.max(peaks[...])

    for cp in pair_copies + rs_copies + ag_copies + fw_copies + peak_copies:
        cp.wait_send()


def shards(sections, tp, head_outputs, residual, out_weight, norm_gain, prior_peak, qkv_weight):
    heads, resid = head_outputs[0], residual[0]
    tokens, depth = heads.shape
    width = out_weight.shape[1]
    columns = qkv_weight.shape[1]
    r = resid.shape[0]
    zs = tp // CORES
    parts = TILE // r
    q = width // parts
    w, v = q // CHUNKS, q // LATE
    bf16, f32 = jnp.bfloat16, jnp.float32
    vmem, hbm, smem = (pl.BlockSpec(memory_space=m) for m in (pltpu.VMEM, pltpu.HBM, pltpu.SMEM))
    dma = pltpu.SemaphoreType.DMA
    flops = 2 * tokens * width * (depth + columns)
    stream, projected, peak = pl.pallas_call(
        functools.partial(kernel, sections, tp),
        out_shape=(
            jax.ShapeDtypeStruct((r, width), bf16),
            jax.ShapeDtypeStruct((tokens, columns), bf16),
            jax.ShapeDtypeStruct((1,), f32),
        ),
        in_specs=[vmem, hbm, hbm, hbm, smem, hbm],
        out_specs=(vmem, vmem, smem),
        scratch_shapes=[
            pltpu.VMEM((tokens, depth), bf16),
            pltpu.VMEM((r, width), bf16),
            pltpu.VMEM((width,), bf16),
            pltpu.VMEM((depth, width), bf16),
            pltpu.VMEM((width, columns), bf16),
            pltpu.VMEM((parts * zs * r, q), f32),
            pltpu.VMEM((CHUNKS, parts * zs * r, w), bf16),
            pltpu.VMEM((CHUNKS, parts * zs * r, w), bf16),
            pltpu.VMEM((CHUNKS, zs, TILE, w), bf16),
            pltpu.VMEM((CHUNKS, zs, TILE, w), bf16),
            pltpu.VMEM((TILE, q), f32),
            pltpu.VMEM((TILE, q), f32),
            pltpu.VMEM((LATE, TILE, v), bf16),
            pltpu.VMEM((LATE, tp, TILE, v), bf16),
            pltpu.VMEM((tp, 8, 128), f32),
            dma, dma, dma((CHUNKS, parts)), dma((LATE, parts)),
            dma((CHUNKS,)), dma((CHUNKS,)),
            dma((CHUNKS, zs)), dma((CHUNKS, zs)),
            dma((LATE, zs)), dma((LATE, zs)),
            dma((LATE, zs)), dma((LATE, zs)),
            dma((tp,)), dma((tp,)),
        ],
        compiler_params=pltpu.CompilerParams(
            collective_id=0, has_side_effects=True, vmem_limit_bytes=VMEM_BYTES),
        cost_estimate=pl.CostEstimate(
            flops=flops, bytes_accessed=2 * width * (depth + columns), transcendentals=0),
    )(heads, pltpu.with_memory_space_constraint(resid, pltpu.HBM), out_weight,
      pltpu.with_memory_space_constraint(norm_gain, pltpu.HBM), prior_peak, qkv_weight)
    return stream[None], projected[None], peak


def solution(mesh):
    sections, tp = mesh.shape["section"], mesh.shape["tp"]
    return jax.shard_map(
        functools.partial(shards, sections, tp),
        mesh=mesh,
        in_specs=(
            P("section", None, "tp"),
            P("section", "tp", None),
            P("tp", None),
            P(),
            P("section"),
            P(None, "tp"),
        ),
        out_specs=(P("section", "tp", None), P("section", None, "tp"), P("section")),
        check_vma=False,
    )
```
